512 devices in a mesh: blk: 16 (over x, y_lo, core), rep: 32 (over z, y_hi).
Axes of the slice: x: 4, y: 4 (y_hi: 2, y_lo: 2; y = y_hi * 2 + y_lo), z: 16, core: 2. Of those that a mesh axis runs over, the one named last changes fastest.
Arguments:
- features: bfloat16 [65536, 256], P(('blk', 'rep')), may hold values from -6 to 6
- weight_one: bfloat16 [256, 256], replicated, may hold values from -0.375 to 0.375
- weight_two: bfloat16 [256, 256], replicated, may hold values from -0.375 to 0.375
- tile_values: bfloat16 [16, 32, 24, 128, 128], P('blk', 'rep'), may hold values from -0.125 to 0.125
- tile_rows: int32 [16, 32, 24], P('blk', 'rep'), may hold values from 0 to 31, as said below
- tile_cols: int32 [16, 32, 24], P('blk', 'rep'), may hold values from 0 to 511, as said below
- tile_count: int32 [16, 32], P('blk', 'rep'), may hold values from 16 to 24, as said below
Outputs:
- aggregated: bfloat16 [65536, 256], P(('blk', 'rep'))
The draws below stay inside these ranges and needn't reach their ends.
Inputs may be any that keep to these rules, and one draw needn't show every extreme that they name: `tile_rows`: block row within the holder's row group into which a tile adds; slots k >= tile_count are ignored. `tile_cols`: A tile held at rep index r has column block j * 32 + r for some j: its columns are nodes held by a device of rep index r. `tile_count`: one device holds exactly 24 live tiles.
All inputs are finite; a program needn't handle non-finite values.
Results may differ from the reference program's by a relative error of at most 0.035.
Values may be sent and summed in bfloat16 or wider, within the bound.
A program may use at most 64 MiB of HBM per device.

```python
import jax
import jax.numpy as jnp
from jax import lax

B = 128
F = 256
BR_DEV = 1
CAP_ROW = 24
CAP = 24
GB = 32
BLOCKS = 512
NODES = 65536
N_BLK = 16
N_REP = 32


def draw_tile_rows(key, part):
    shape_all = (N_BLK, N_REP, CAP)
    offset = jax.random.randint(jax.random.fold_in(key, 11), (N_BLK, N_REP, 1), 0, GB, dtype=jnp.int32)
    stride = 1 + 2 * jax.random.randint(jax.random.fold_in(key, 12), (N_BLK, N_REP, 1), 0, GB, dtype=jnp.int32)
    slot_ids = lax.broadcasted_iota(jnp.int32, shape_all, 2)
    return ((offset + slot_ids * stride) % GB).astype(jnp.int32)


def draw_tile_cols(key, part):
    shape_all = (N_BLK, N_REP, CAP)
    group_pick = jax.random.randint(jax.random.fold_in(key, 21), shape_all, 0, N_BLK, dtype=jnp.int32)
    sub_pick = jax.random.randint(jax.random.fold_in(key, 22), shape_all, 0, BR_DEV, dtype=jnp.int32)
    slot_ids = lax.broadcasted_iota(jnp.int32, shape_all, 1)
    return (group_pick * N_REP + slot_ids) * BR_DEV + sub_pick


def draw_tile_count(key, part):
    base_count = CAP - CAP // 3
    level = jax.random.randint(jax.random.fold_in(key, 31), (N_BLK, N_REP), 0, CAP, dtype=jnp.int32)
    counted = base_count + level * (CAP - base_count) // CAP
    total_devs = N_BLK * N_REP
    chosen = jax.random.randint(jax.random.fold_in(key, 32), (), 0, total_devs, dtype=jnp.int32)
    lowest = (chosen + 1) % total_devs
    flat_ids = lax.broadcasted_iota(jnp.int32, (N_BLK, N_REP), 0) * N_REP + lax.broadcasted_iota(jnp.int32, (N_BLK, N_REP), 1)
    counted = jnp.where(flat_ids == lowest, base_count, counted)
    return jnp.where(flat_ids == chosen, CAP, counted).astype(jnp.int32)


def levels(key, shape, split, low, top_value):
    factor_of, own = 1.0, jax.random.fold_in(key, 6)
    for position, parts in split:
        steps = jnp.exp(jax.random.uniform(jax.random.fold_in(own, position), (parts,), jnp.float32, low / len(split), top_value / len(split)))
        factor_of = factor_of * jnp.repeat(steps, shape[position] // parts).reshape([-1 if axis == position else 1 for axis in range(len(shape))])
    return factor_of


def bell_draw(stream_key, extent, deviation, most, split=(), kind=jnp.bfloat16):
    factor_of = levels(stream_key, extent, split, -0.22, 0.18) if split else 1.0
    entries = jax.random.normal(stream_key, extent, jnp.float32) * deviation * factor_of
    return jnp.minimum(jnp.maximum(entries, -most), most).astype(kind)


def setup_inputs(seed: int = 0) -> dict:
    key_list = jax.random.split(jax.random.key(seed), 8)
    return {
        "features": bell_draw(key_list[0], (NODES, F), 1.0, 6.0, ((0, 512),)),
        "weight_one": bell_draw(key_list[1], (F, F), F ** -0.5, 0.375),
        "weight_two": bell_draw(key_list[2], (F, F), F ** -0.5, 0.375),
        "tile_values": bell_draw(key_list[3], (N_BLK, N_REP, CAP, B, B), (CAP_ROW * B * 2 // 3) ** -0.5, 0.125, ((0, 16), (1, 32))),
        "tile_rows": draw_tile_rows(jax.random.fold_in(key_list[7], 71), 0),
        "tile_cols": draw_tile_cols(jax.random.fold_in(key_list[7], 71), 0),
        "tile_count": draw_tile_count(jax.random.fold_in(key_list[7], 71), 0),
    }


def aggregate(panel_rows, tile_values, tile_rows, tile_cols, tile_count):
    node_blocks = panel_rows.reshape(BLOCKS, B, F)
    slot_ids = jnp.arange(CAP).astype(jnp.int32)
    group_ids = jnp.arange(GB).astype(jnp.int32)

    def one_device(unused, inputs):
        tile_vals, row_ids, col_ids, live_count = inputs
        source = node_blocks[col_ids.astype(jnp.int32)]
        products = jnp.einsum("kab,kbf->kaf", tile_vals.astype(jnp.float32), source.astype(jnp.float32), precision=lax.Precision.HIGHEST)
        placing = ((row_ids[:, None] == group_ids[None, :]) & (slot_ids < live_count)[:, None]).astype(jnp.float32)
        partial_value = jnp.einsum("kg,kaf->gaf", placing, products, precision=lax.Precision.HIGHEST)
        return unused, partial_value.astype(jnp.bfloat16)

    def one_group(unused, inputs):
        unused_two, slot_parts = lax.scan(one_device, unused, inputs)
        return unused, jnp.sum(slot_parts.astype(jnp.float32), axis=0)

    unused_end, group_sums = lax.scan(one_group, jnp.float32(0.0), (tile_values, tile_rows, tile_cols, tile_count))
    return group_sums.reshape(NODES, F)


def reference(features, weight_one, weight_two, tile_values, tile_rows, tile_cols, tile_count):
    panel_one = jnp.dot(features, weight_one, preferred_element_type=jnp.float32).astype(jnp.bfloat16)
    sum_one = aggregate(panel_one, tile_values, tile_rows, tile_cols, tile_count)
    hidden = jnp.maximum(sum_one, 0.0).astype(jnp.bfloat16)
    panel_two = jnp.dot(hidden, weight_two, preferred_element_type=jnp.float32).astype(jnp.bfloat16)
    sum_two = aggregate(panel_two, tile_values, tile_rows, tile_cols, tile_count)
    return sum_two.astype(jnp.bfloat16)
```

```python
import functools

import jax
import jax.numpy as jnp
from jax import lax
from jax.experimental import pallas as pl
from jax.experimental.pallas import tpu as pltpu
from jax.sharding import PartitionSpec as P

MESH = pl.DeviceIdType.MESH
NX, NY, NC = 4, 2, 2
NZ, NH = 16, 2
NB = NX * NY * NC
B, F, FH, CAP, GB = 128, 256, 128, 24, 32
HALF = NZ // 2
PIECES = 4
SLOTS = HALF + 1
PEERS = [(0, 1), (1, 0), (3, 0), (1, 1), (3, 1), (2, 0), (2, 1)]
BF, F32 = jnp.bfloat16, jnp.float32


def kernel(
    feat_hbm, w1_hbm, w2_hbm, tiles_hbm, rows_hbm, cols_hbm, count_hbm, out_ref,
    feat, w1, w2, tiles, rows, cols, count, rowm, prev, last,
    g00, g01, g10, g11, s0, s1, rbuf, own, hid, ysend, yrecv,
    in_sem, gsend, grecv, csend, crecv, ysend_sem, yrecv_sem,
):
    b, r = lax.axis_index("blk"), lax.axis_index("rep")
    core, ylo, x = lax.rem(b, NC), lax.rem(lax.div(b, NC), NY), lax.div(b, NC * NY)
    yhi, z = lax.rem(r, NH), lax.div(r, NH)

    def blk_at(dx, dy, dc):
        return (lax.rem(x + dx, NX) * NY + lax.rem(ylo + dy, NY)) * NC + lax.rem(core + dc, NC)

    up, down = lax.rem(z + 1, NZ) * NH + yhi, lax.rem(z + NZ - 1, NZ) * NH + yhi
    z_peer = (up, down)
    y_peer = z * NH + 1 - yhi
    sibling = blk_at(0, 0, 1)

    loads = [
        pltpu.make_async_copy(src, dst, in_sem.at[i])
        for i, (src, dst) in enumerate((
            (feat_hbm, feat), (w1_hbm, w1), (rows_hbm, rows), (cols_hbm, cols),
            (count_hbm, count), (tiles_hbm, tiles), (w2_hbm, w2),
        ))
    ]
    for load in loads:
        load.start()

    barrier = pltpu.get_barrier_semaphore()
    for dx, dy in PEERS:
        pl.semaphore_signal(barrier, inc=1, device_id=(blk_at(dx, dy, 0), r), device_id_type=MESH)
    pl.semaphore_signal(barrier, inc=1, device_id=(sibling, r), device_id_type=MESH)
    for peer in (up, down, y_peer):
        pl.semaphore_signal(barrier, inc=1, device_id=(b, peer), device_id_type=MESH)

    gath = ((g00, g01), (g10, g11))
    sums = (s0, s1)
    for s_ref in sums:
        s_ref[0] = jnp.zeros((B, FH), F32)

    def landed(ref, sem):
        pltpu.make_async_copy(ref, ref, sem).wait()

    def gather_copy(layer, half, slot, to):
        g = gath[layer][half]
        return pltpu.make_async_remote_copy(
            src_ref=g.at[slot], dst_ref=g.at[slot], send_sem=gsend.at[layer, half],
            recv_sem=grecv.at[layer, half, slot], device_id=(to, r), device_id_type=MESH,
        )

    def gather_start(layer, half):
        for dx, dy in PEERS:
            gather_copy(layer, half, b, blk_at(dx, dy, 0)).start()
        gather_copy(layer, half, b, sibling).start()

    def gather_finish(layer, half):
        g = gath[layer][half]
        for dx, dy in PEERS:
            source = blk_at(NX - dx, dy, 0)
            landed(g.at[source], grecv.at[layer, half, source])
            gather_copy(layer, half, source, sibling).start()
        for dx, dy in [(0, 0), *PEERS]:
            source = blk_at(NX - dx, dy, 1)
            landed(g.at[source], grecv.at[layer, half, source])

    def meta():
        for load in loads[2:5]:
            load.wait()
        live = count[0, 0]
        for k in range(CAP):
            rowm[k] = jnp.where(k < live, rows[0, 0, k], -1)

        def prev_of(k, carry):
            mine, found = rowm[k], jnp.int32(0)
            for j in range(CAP - 1):
                found = jnp.where((rowm[j] == mine) & (j < k), j + 1, found)
            prev[k] = found
            return carry

        lax.fori_loop(0, CAP, prev_of, 0)

        def last_of(g, carry):
            found = jnp.int32(0)
            for j in range(CAP):
                found = jnp.where(rowm[j] == g, j + 1, found)
            last[g] = found
            return carry

        lax.fori_loop(0, GB, last_of, 0)

    def products(layer, half):
        g, s_ref = gath[layer][half], sums[half]
        for k in range(CAP):
            block = g[cols[0, 0, k] // GB]
            s_ref[k + 1] = jnp.dot(tiles[0, 0, k], block, preferred_element_type=F32)

        def add(k, carry):
            s_ref[k + 1] = s_ref[k + 1] + s_ref[prev[k]]
            return carry

        lax.fori_loop(0, CAP, add, 0)

    def partial_of(target, piece):
        y = 1 - yhi if piece % 2 == 0 else yhi
        return sums[piece // 2][last[target * NH + y]]

    def target_at(d, step):
        return lax.rem(z + (HALF - step if d == 0 else HALF + step), NZ)

    def send_piece(layer, d, step, piece):
        pltpu.make_async_remote_copy(
            src_ref=rbuf.at[layer, d * SLOTS + step, piece],
            dst_ref=rbuf.at[layer, d * SLOTS + step + 1, piece],
            send_sem=csend.at[layer],
            recv_sem=crecv.at[layer, d * SLOTS + step + 1, piece],
            device_id=(b, z_peer[d]), device_id_type=MESH,
        ).start()

    def first_sends(layer, half):
        for step in range(2):
            for piece in (2 * half, 2 * half + 1):
                d = (piece + step) % 2
                rbuf[layer, d * SLOTS + step, piece] = partial_of(target_at(d, step), piece).astype(BF)
                send_piece(layer, d, step, piece)

    def chain_piece(layer, d, step, piece):
        slot = d * SLOTS + step
        landed(rbuf.at[layer, slot, piece], crecv.at[layer, slot, piece])
        total = rbuf[layer, slot, piece].astype(F32) + partial_of(target_at(d, step), piece)
        rbuf[layer, slot, piece] = total.astype(BF)
        send_piece(layer, d, step, piece)

    def y_copy(layer, half):
        return pltpu.make_async_remote_copy(
            src_ref=ysend.at[layer, half], dst_ref=yrecv.at[layer, half],
            send_sem=ysend_sem.at[layer, half], recv_sem=yrecv_sem.at[layer, half],
            device_id=(b, y_peer), device_id_type=MESH,
        )

    def reduce_scatter(layer):
        for piece in range(PIECES):
            chain_piece(layer, piece % 2, 1, piece)

        def step_body(step, carry):
            for piece in range(PIECES):
                for d in range(2):
                    chain_piece(layer, d, step, piece)
            return carry

        lax.fori_loop(2, HALF, step_body, 0)
        for piece in range(PIECES):
            total = partial_of(z, piece)
            for d in range(2):
                slot = d * SLOTS + HALF
                landed(rbuf.at[layer, slot, piece], crecv.at[layer, slot, piece])
                total += rbuf[layer, slot, piece].astype(F32)
            half = piece // 2
            if piece % 2 == 0:
                ysend[layer, half] = total.astype(BF)
                y_copy(layer, half).start()
            else:
                own[half] = total
        for half in range(2):
            y_copy(layer, half).wait_recv()
            total = own[half] + yrecv[layer, half].astype(F32)
            columns = pl.ds(half * FH, FH)
            if layer == 0:
                hid[:, columns] = jnp.maximum(total, 0.0).astype(BF)
            else:
                out_ref[:, columns] = total.astype(BF)

    for layer in range(2):
        if layer == 0:
            loads[0].wait()
            loads[1].wait()
        else:
            loads[6].wait()
        panel = jnp.dot(
            (feat, hid)[layer][...], (w1, w2)[layer][...], preferred_element_type=F32
        ).astype(BF)
        for half in range(2):
            gath[layer][half][b] = panel[:, half * FH : (half + 1) * FH]
        if layer == 0:
            pl.semaphore_wait(barrier, len(PEERS) + 4)
        for half in range(2):
            gather_start(layer, half)
        if layer == 0:
            meta()
            loads[5].wait()
        for half in range(2):
            gather_finish(layer, half)
            products(layer, half)
            first_sends(layer, half)
        reduce_scatter(layer)

    for layer in range(2):
        for half in range(2):
            landed(gath[layer][half].at[pl.ds(0, NB - 1)], gsend.at[layer, half])
            y_copy(layer, half).wait_send()
        landed(rbuf.at[layer, pl.ds(0, NZ - 1)], csend.at[layer])


def body(*args):
    vmem = pltpu.VMEM
    dma = pltpu.SemaphoreType.DMA
    return pl.pallas_call(
        kernel,
        out_shape=jax.ShapeDtypeStruct((B, F), BF),
        in_specs=[pl.BlockSpec(memory_space=pl.ANY)] * 7,
        out_specs=pl.BlockSpec(memory_space=pltpu.VMEM),
        scratch_shapes=[
            vmem((B, F), BF), vmem((F, F), BF), vmem((F, F), BF), vmem((1, 1, CAP, B, B), BF),
            pltpu.SMEM((1, 1, CAP), jnp.int32), pltpu.SMEM((1, 1, CAP), jnp.int32), pltpu.SMEM((1, 1), jnp.int32),
            pltpu.SMEM((CAP,), jnp.int32), pltpu.SMEM((CAP,), jnp.int32), pltpu.SMEM((GB,), jnp.int32),
            *[vmem((NB, B, FH), BF)] * 4,
            *[vmem((CAP + 1, B, FH), F32)] * 2,
            vmem((2, 2 * SLOTS, PIECES, B, FH), BF),
            vmem((2, B, FH), F32), vmem((B, F), BF),
            vmem((2, 2, B, FH), BF), vmem((2, 2, B, FH), BF),
            dma((7,)), dma((2, 2)), dma((2, 2, NB)),
            dma((2,)), dma((2, 2 * SLOTS, PIECES)), dma((2, 2)), dma((2, 2)),
        ],
        compiler_params=pltpu.CompilerParams(
            collective_id=0, has_side_effects=True, vmem_limit_bytes=40 * 2**20
        ),
        cost_estimate=pl.CostEstimate(
            flops=2 * CAP * 2 * B * B * F + 4 * B * F * F, bytes_accessed=2**21, transcendentals=0
        ),
    )(*args)


def solution(mesh):
    in_specs = (
        P(("blk", "rep"), None),
        P(),
        P(),
        P("blk", "rep", None, None, None),
        P("blk", "rep", None),
        P("blk", "rep", None),
        P("blk", "rep"),
    )
    out_specs = P(("blk", "rep"), None)
    return jax.shard_map(body, mesh=mesh, in_specs=in_specs, out_specs=out_specs, check_vma=False)
```
